256 devices in a mesh: row: 4 (over y), col: 64 (over z, x, core).
Axes of the slice: x: 4, y: 4, z: 8, core: 2. Of those that a mesh axis runs over, the one named last changes fastest.
Arguments:
- amplitudes: bfloat16 [512, 512, 512], P('col', None, 'row'), may hold values from -16 to 16
- integrals: bfloat16 [512, 1, 512, 512], P(None, None, 'col', 'row'), may hold values from -0.0625 to 0.0625
- virtual_irrep: int32 [512], replicated, may hold values from 0 to 3, as said below
- pair_irrep: int32 [512], replicated, may hold values from 0 to 3, as said below
Outputs:
- residual: float32 [512, 1, 512], P('col', None, 'row')
The draws below stay inside these ranges and needn't reach their ends.
Inputs may be any that keep to these rules, and one draw needn't show every extreme that they name: `virtual_irrep`: orbitals are sorted by irrep: labels never fall along the orbitals, and each of the 4 irreps is one contiguous run of at least 64 orbitals. `pair_irrep`: pairs are sorted by irrep: labels never fall along the pairs, and each of the 4 irreps is one contiguous run of at least 64 pairs.
All inputs are finite; a program needn't handle non-finite values.
Results may differ from the reference program's by a relative error of at most 0.0003.
Values may be sent and summed in bfloat16 or wider, within the bound.
A program may use at most 64 MiB of HBM per device.

```python
import jax
import jax.numpy as jnp
from jax import lax

NV = 512
NIRR = 4
A_SLAB = 1
PAIRS = 512


def sorted_labels(key, total):
    least = total // 8
    cuts = jnp.sort(jax.random.randint(key, (NIRR - 1,), 0, total - NIRR * least + 1))
    bounds = cuts + least * jnp.arange(1, NIRR, dtype=jnp.int32)
    places = jnp.arange(total, dtype=jnp.int32)
    return jnp.sum((places[:, None] >= bounds[None, :]).astype(jnp.int32), axis=1).astype(jnp.int32)


def draw_virtual_irrep(key, part):
    key = jax.random.fold_in(key, 11)
    return sorted_labels(key, NV)


def draw_pair_irrep(key, part):
    key = jax.random.fold_in(key, 23)
    return sorted_labels(key, PAIRS)


def raised(values, own_key, source, target, shards_of, factor):
    def block_of(position):
        return (jnp.arange(values.shape[position]) // (values.shape[position] // shards_of)).reshape((-1,) + (1,) * (values.ndim - 1 - position))

    first = jax.random.permutation(own_key, shards_of)[block_of(target)]
    second = (block_of(target) + shards_of // 2) % shards_of
    return jnp.where((block_of(source) == first) | (block_of(source) == second), factor * values, values)


def steps_of(own_key, extent, split, smallest, largest):
    def one(axis_at, shards_of):
        draws = jax.random.uniform(jax.random.fold_in(jax.random.fold_in(own_key, 6), axis_at), (shards_of,), jnp.float32, smallest / len(split), largest / len(split))
        return jnp.repeat(jnp.exp(draws), extent[axis_at] // shards_of).reshape((-1,) + (1,) * (len(extent) - axis_at - 1))

    gain = one(*split[0])
    for cut in split[1:]:
        gain = gain * one(*cut)
    return gain


def heavy_noise(stream_key, shape, width, limit, shards, heavy, kind=jnp.bfloat16):
    array = width * jax.random.normal(stream_key, shape, jnp.float32)
    if shards:
        array = array * steps_of(stream_key, shape, shards, -0.22, 0.18)
    return jnp.clip(raised(array, jax.random.fold_in(stream_key, 3), *heavy), -limit, limit).astype(kind)


def setup_inputs(seed: int = 0) -> dict:
    keys = jax.random.split(jax.random.key(seed), 5)
    amplitudes = heavy_noise(keys[0], (PAIRS, NV, NV), 1.0, 16.0, ((0, 64), (2, 4)), (2, 0, 64, 4.0))
    integrals = heavy_noise(keys[1], (NV, A_SLAB, NV, NV), (NV * NV // 4) ** -0.5, 0.0625, ((2, 64), (3, 4)), (2, 0, 64, 4.0))
    virtual_irrep = draw_virtual_irrep(jax.random.fold_in(keys[4], 71), 0)
    pair_irrep = draw_pair_irrep(jax.random.fold_in(keys[4], 71), 0)
    return dict(amplitudes=amplitudes, integrals=integrals, virtual_irrep=virtual_irrep, pair_irrep=pair_irrep)


def reference(amplitudes, integrals, virtual_irrep, pair_irrep):
    sym_dc = jnp.bitwise_xor(virtual_irrep[:, None], virtual_irrep[None, :])
    keep = pair_irrep[:, None, None] == sym_dc[None, :, :]
    masked_amp = jnp.where(keep, amplitudes, jnp.zeros_like(amplitudes))
    flat_amp = masked_amp.reshape(PAIRS, NV * NV)
    block = 8
    blocks = integrals.reshape(NV // block, block * A_SLAB, NV * NV)

    def one_block(slab):
        return jnp.dot(slab, flat_amp.T, preferred_element_type=jnp.float32)

    term = lax.map(one_block, blocks).reshape(NV, A_SLAB, PAIRS)
    sym_ba = jnp.bitwise_xor(virtual_irrep[:, None], virtual_irrep[None, :A_SLAB])
    live = sym_ba[:, :, None] == pair_irrep[None, None, :]
    return jnp.where(live, term, jnp.zeros_like(term))
```

```python
import functools

import jax
import jax.numpy as jnp
from jax import lax
from jax.experimental import pallas as pl
from jax.experimental.pallas import tpu as pltpu
from jax.sharding import PartitionSpec as P

MESH = pl.DeviceIdType.MESH
F32 = jnp.float32
BF16 = jnp.bfloat16
NZ, NX, NY = 8, 4, 4
CHIPS = NZ * NX
LANES = 128
IRREPS = 4


def kernel(
    t_hbm, v_hbm, virt_ref, pair_ref, out_ref,
    recv, vbuf, vf, vmat, tf, tmat, sbuf, s1, msg, fin,
    tsend, trecv, vsem, ssend, srecv, msend, mrecv,
):
    row = lax.axis_index("row")
    col = lax.axis_index("col")
    core = lax.rem(col, 2)
    chip = lax.div(col, 2)
    z = lax.div(chip, NX)
    x = lax.rem(chip, NX)
    other = 1 - core

    def shifted(t):
        return lax.rem(z + lax.div(t, NX), NZ) * NX + lax.rem(x + lax.rem(t, NX), NX)

    def here(chip_index, core_index):
        return {"row": row, "col": chip_index * 2 + core_index}

    barrier = pltpu.get_barrier_semaphore()

    def greet(t, carry):
        pl.semaphore_signal(barrier, inc=1, device_id=here(shifted(t), core), device_id_type=MESH)
        return carry

    lax.fori_loop(1, CHIPS, greet, 0)
    pl.semaphore_signal(barrier, inc=1, device_id=here(chip, other), device_id_type=MESH)
    for hop in range(1, NY):
        for c in range(2):
            pl.semaphore_signal(
                barrier, inc=1, device_id={"row": lax.rem(row + hop, NY), "col": chip * 2 + c}, device_id_type=MESH
            )
    pl.semaphore_wait(barrier, CHIPS - 1 + 1 + 2 * (NY - 1))

    def chunk(target):
        return pltpu.make_async_remote_copy(
            src_ref=t_hbm.at[:, pl.ds(pl.multiple_of(target * 16, 16), 16), :],
            dst_ref=recv.at[chip],
            send_sem=tsend.at[target],
            recv_sem=trecv.at[chip],
            device_id=here(target, core),
            device_id_type=MESH,
        )

    def send(t, carry):
        chunk(shifted(t)).start()
        return carry

    lax.fori_loop(1, CHIPS, send, 0)
    own_t = pltpu.make_async_copy(
        t_hbm.at[:, pl.ds(pl.multiple_of(chip * 16, 16), 16), :], recv.at[chip], trecv.at[chip]
    )
    own_t.start()

    own_v = pltpu.make_async_copy(v_hbm, vbuf.at[0], vsem.at[0])
    own_v.start()
    give_v = pltpu.make_async_remote_copy(
        src_ref=v_hbm, dst_ref=vbuf.at[1], send_sem=vsem.at[1], recv_sem=vsem.at[2],
        device_id=here(chip, other), device_id_type=MESH,
    )
    give_v.start()

    labels = virt_ref[...]
    starts = []
    for n in range(1, IRREPS):
        below = jnp.where(labels < n, 1.0, 0.0).astype(F32)
        starts.append(jnp.sum(jnp.sum(below, axis=1, keepdims=True), axis=0, keepdims=True))

    def label_of(place):
        place = place.astype(F32)
        total = jnp.zeros(place.shape, jnp.int32)
        for start in starts:
            total = total + jnp.where(place >= start, 1, 0)
        return total

    irrep_a = label_of(jnp.zeros((1, LANES), jnp.int32))
    irrep_c = virt_ref[pl.ds(row, 1), :]
    irrep_b = label_of(lax.broadcasted_iota(jnp.int32, (512, LANES), 0))

    def lay_v(half, from_core):
        def widen(i, carry):
            rows = pl.ds(pl.multiple_of(i * 512, 512), 512)
            vf[rows, :] = vbuf[half, rows, :].astype(F32)
            return carry

        lax.fori_loop(0, 8, widen, 0)

        for d in range(8):
            place = chip * 16 + from_core * 8 + d
            irrep_d = label_of(jnp.full((1, LANES), 1, jnp.int32) * place)
            want = jnp.bitwise_xor(jnp.bitwise_xor(irrep_d, irrep_c), irrep_a)
            value = vf[pl.ds(d, 512, stride=8), :]
            value = jnp.where(irrep_b == want, value, 0.0)
            value = value.reshape(CHIPS, 2, 8, LANES)
            lanes = pl.ds(pl.multiple_of((from_core * 8 + d) * LANES, LANES), LANES)
            for c in range(2):
                vmat[c * 256 : c * 256 + 256, lanes] = value[:, c].reshape(256, LANES).astype(BF16)

    own_v.wait()
    lay_v(0, core)
    give_v.wait()
    lay_v(1, other)

    lane = lax.broadcasted_iota(jnp.int32, (LANES, LANES), 1)
    low = (lane < 64) == (core == 0)

    def s1_copy(q, c):
        return pltpu.make_async_remote_copy(
            src_ref=sbuf.at[q, c],
            dst_ref=s1.at[2 * row + core],
            send_sem=ssend.at[q, c],
            recv_sem=srecv.at[2 * row + core],
            device_id={"row": q, "col": chip * 2 + c},
            device_id_type=MESH,
        )

    def quarter(step, carry):
        q = lax.rem(lax.div(z, 2) + step, NY)

        def arrived(i, inner):
            source = q * 8 + i
            pltpu.make_async_copy(recv.at[source], recv.at[source], trecv.at[source]).wait()
            return inner

        lax.fori_loop(0, 8, arrived, 0)
        tf[...] = recv[pl.ds(q * 8, 8)].reshape(1024, LANES).astype(F32)
        for d in range(16):
            value = tf[pl.ds(d, 64, stride=16), :].astype(BF16)
            tmat[0:64, d * LANES : (d + 1) * LANES] = value
            tmat[64:128, d * LANES : (d + 1) * LANES] = value
        for c in range(2):
            product = lax.dot_general(
                vmat[c * 256 : c * 256 + 256, :], tmat[...], (((1,), (1,)), ((), ())), preferred_element_type=F32
            )
            packed = jnp.where(low, product[:128], product[128:])
            mine = jnp.logical_and(q == row, core == c)

            @pl.when(mine)
            def _():
                s1[2 * row + core] = packed

            @pl.when(jnp.logical_not(mine))
            def _():
                sbuf[q, c] = packed
                s1_copy(q, c).start()

        return carry

    lax.fori_loop(0, NY, quarter, 0)

    me = 2 * row + core

    def s1_wait(i, carry):
        slot = lax.rem(me + i, 8)
        pltpu.make_async_copy(s1.at[slot], s1.at[slot], srecv.at[slot]).wait()
        return carry

    lax.fori_loop(1, 8, s1_wait, 0)
    from0 = s1[0] + s1[2] + s1[4] + s1[6]
    from1 = s1[1] + s1[3] + s1[5] + s1[7]
    first = lane < 64
    msg[0:16] = jnp.where(first, from0, from1).reshape(16, 8, LANES)
    msg[16:32] = jnp.where(first, from1, from0).reshape(16, 8, LANES)

    def block(target):
        return pltpu.make_async_remote_copy(
            src_ref=msg.at[target], dst_ref=fin.at[chip], send_sem=msend.at[target], recv_sem=mrecv.at[chip],
            device_id=here(target, core), device_id_type=MESH,
        )

    def give(t, carry):
        block(shifted(t)).start()
        return carry

    lax.fori_loop(1, CHIPS, give, 0)
    fin[chip] = msg[chip]

    def taken(t, carry):
        source = shifted(t)
        pltpu.make_async_copy(fin.at[source], fin.at[source], mrecv.at[source]).wait()
        return carry

    lax.fori_loop(1, CHIPS, taken, 0)
    total = fin[0]
    for i in range(1, CHIPS):
        total = total + fin[i]

    source = lax.broadcasted_iota(jnp.int32, (LANES, LANES), 0)
    half = jnp.where(source < 64, 0, 1)
    source_core = jnp.where(chip < 16, half, 1 - half)
    inside = source - 64 * half
    target = 16 * lax.div(inside, 8) + 8 * source_core + lax.rem(inside, 8)
    move = jnp.where(target == lane, 1.0, 0.0).astype(F32)
    result = lax.dot_general(
        total, move, (((1,), (0,)), ((), ())), preferred_element_type=F32, precision=lax.Precision.HIGHEST
    )
    irrep_b8 = label_of(col * 8 + lax.broadcasted_iota(jnp.int32, (8, LANES), 0))
    live = jnp.bitwise_xor(irrep_b8, irrep_a) == pair_ref[pl.ds(row, 1), :]
    out_ref[...] = jnp.where(live, result, 0.0)

    def t_left(t, carry):
        chunk(shifted(t)).wait_send()
        block(shifted(t)).wait_send()
        return carry

    lax.fori_loop(1, CHIPS, t_left, 0)

    def s_left(i, carry):
        slot = lax.rem(me + i, 8)
        s1_copy(lax.div(slot, 2), lax.rem(slot, 2)).wait_send()
        return carry

    lax.fori_loop(1, 8, s_left, 0)


def on_device(amplitudes, integrals, virtual_irrep, pair_irrep):
    pairs, span_d, span_c = amplitudes.shape
    v = integrals.reshape(512 * 8, LANES)
    hbm = pl.BlockSpec(memory_space=pl.ANY)
    vmem = pl.BlockSpec(memory_space=pltpu.VMEM)
    out = pl.pallas_call(
        kernel,
        out_shape=jax.ShapeDtypeStruct((8, LANES), F32),
        in_specs=[hbm, hbm, vmem, vmem],
        out_specs=vmem,
        scratch_shapes=[
            pltpu.VMEM((CHIPS, 8, 16, LANES), BF16),
            pltpu.VMEM((2, 4096, LANES), BF16),
            pltpu.VMEM((4096, LANES), F32),
            pltpu.VMEM((512, 2048), BF16),
            pltpu.VMEM((1024, LANES), F32),
            pltpu.VMEM((128, 2048), BF16),
            pltpu.VMEM((4, 2, 128, LANES), F32),
            pltpu.VMEM((8, 128, LANES), F32),
            pltpu.VMEM((CHIPS, 8, LANES), F32),
            pltpu.VMEM((CHIPS, 8, LANES), F32),
            pltpu.SemaphoreType.DMA((CHIPS,)),
            pltpu.SemaphoreType.DMA((CHIPS,)),
            pltpu.SemaphoreType.DMA((3,)),
            pltpu.SemaphoreType.DMA((4, 2)),
            pltpu.SemaphoreType.DMA((8,)),
            pltpu.SemaphoreType.DMA((CHIPS,)),
            pltpu.SemaphoreType.DMA((CHIPS,)),
        ],
        compiler_params=pltpu.CompilerParams(
            collective_id=0, has_side_effects=True, vmem_limit_bytes=32 * 1024 * 1024
        ),
        name="ladder",
    )(amplitudes, v, virtual_irrep.reshape(4, LANES), pair_irrep.reshape(4, LANES))
    return out.reshape(8, 1, LANES)


def solution(mesh):
    in_specs = (P("col", None, "row"), P(None, None, "col", "row"), P(), P())
    out_specs = P("col", None, "row")
    return jax.shard_map(on_device, mesh=mesh, in_specs=in_specs, out_specs=out_specs, check_vma=False)
```

```python
import jax
import jax.numpy as jnp
from jax import lax
from jax.experimental import pallas as pl
from jax.experimental.pallas import tpu as pltpu
from jax.sharding import PartitionSpec as P

MESH = pl.DeviceIdType.MESH
F32 = jnp.float32
BF16 = jnp.bfloat16
NZ, NX, NY = 8, 4, 4
CHIPS = NZ * NX
LANES = 128
IRREPS = 4
Z_ORDER = (4, 5, 6, 7, 2, 3, 1, 0)
X_ORDER = (2, 1, 3, 0)


def flip(value, mask, bits):
    total = 0
    for bit in range(bits):
        one = lax.rem(lax.div(value, 1 << bit), 2)
        total = total + (1 << bit) * (1 - one if mask >> bit & 1 else one)
    return total


def kernel(
    t_hbm, v_hbm, virt_hbm, pair_hbm, out_ref,
    tsrc, virt_ref, pair_ref, recv, vbuf, vf, vmat, tf, tmat, sbuf, s1, msg, fin,
    lsem, tsend, trecv, vsem, ssend, srecv, msend, mrecv,
):
    row = lax.axis_index("row")
    col = lax.axis_index("col")
    core = lax.rem(col, 2)
    chip = lax.div(col, 2)
    z = lax.div(chip, NX)
    x = lax.rem(chip, NX)
    other = 1 - core

    loads = [
        pltpu.make_async_copy(t_hbm, tsrc, lsem.at[0]),
        pltpu.make_async_copy(virt_hbm, virt_ref, lsem.at[1]),
        pltpu.make_async_copy(pair_hbm, pair_ref, lsem.at[2]),
        pltpu.make_async_copy(v_hbm, vbuf.at[0], vsem.at[0]),
    ]
    for load in loads:
        load.start()

    def around(dx):
        return lax.rem(x + dx, NX)

    def at(z_index, x_index, core_index, row_index):
        return {"row": row_index, "col": (z_index * NX + x_index) * 2 + core_index}

    plane = [(flip(z, m, 3), around(dx)) for m in Z_ORDER for dx in X_ORDER if (m, dx) != (0, 0)]
    block_mates = [(dx, dc, dy) for dy in range(NY) for dx in X_ORDER for dc in range(2)]

    barrier = pltpu.get_barrier_semaphore()
    met = 0
    for tz, tx in plane:
        pl.semaphore_signal(barrier, inc=1, device_id=at(tz, tx, core, row), device_id_type=MESH)
        met += 1
    for dx, dc, dy in block_mates:
        if dc == 0 and dy == 0:
            continue
        mate = at(z, around(dx), lax.rem(core + dc, 2), lax.rem(row + dy, NY))
        pl.semaphore_signal(barrier, inc=1, device_id=mate, device_id_type=MESH)
        met += 1
    loads[0].wait()
    pl.semaphore_wait(barrier, met)

    def chunk(tz, tx):
        target = tz * NX + tx
        return pltpu.make_async_remote_copy(
            src_ref=tsrc.at[:, pl.ds(pl.multiple_of(target * 16, 16), 16), :],
            dst_ref=recv.at[chip],
            send_sem=tsend.at[target],
            recv_sem=trecv.at[chip],
            device_id=at(tz, tx, core, row),
            device_id_type=MESH,
        )

    chunks = [chunk(tz, tx) for tz, tx in plane]
    for copy in chunks:
        copy.start()
    own_t = pltpu.make_async_copy(
        tsrc.at[:, pl.ds(pl.multiple_of(chip * 16, 16), 16), :], recv.at[chip], trecv.at[chip]
    )
    own_t.start()
    give_v = pltpu.make_async_remote_copy(
        src_ref=v_hbm, dst_ref=vbuf.at[1], send_sem=vsem.at[1], recv_sem=vsem.at[2],
        device_id=at(z, x, other, row), device_id_type=MESH,
    )
    give_v.start()

    loads[1].wait()
    loads[2].wait()
    labels = virt_ref[...]
    starts = []
    for n in range(1, IRREPS):
        below = jnp.where(labels < n, 1.0, 0.0).astype(F32)
        starts.append(jnp.sum(jnp.sum(below, axis=1, keepdims=True), axis=0, keepdims=True))

    def label_of(place):
        place = place.astype(F32)
        total = jnp.zeros(place.shape, jnp.int32)
        for start in starts:
            total = total + jnp.where(place >= start, 1, 0)
        return total

    irrep_a = label_of(jnp.zeros((1, LANES), jnp.int32))
    irrep_c = virt_ref[pl.ds(row, 1), :]
    irrep_b = label_of(lax.broadcasted_iota(jnp.int32, (512, LANES), 0))

    def lay_v(half, from_core):
        def widen(i, carry):
            rows = pl.ds(pl.multiple_of(i * 512, 512), 512)
            vf[rows, :] = vbuf[half, rows, :].astype(F32)
            return carry

        lax.fori_loop(0, 8, widen, 0)

        for d in range(8):
            place = chip * 16 + from_core * 8 + d
            irrep_d = label_of(jnp.full((1, LANES), 1, jnp.int32) * place)
            want = jnp.bitwise_xor(jnp.bitwise_xor(irrep_d, irrep_c), irrep_a)
            value = vf[pl.ds(d, 512, stride=8), :]
            value = jnp.where(irrep_b == want, value, 0.0)
            value = value.reshape(2, 4, NX, 2, 8, LANES)
            lanes = pl.ds(pl.multiple_of((from_core * 8 + d) * LANES, LANES), LANES)
            for h in range(2):
                for tx in range(NX):
                    for c in range(2):
                        at_row = h * 256 + (tx * 2 + c) * 32
                        vmat[at_row : at_row + 32, lanes] = value[h, :, tx, c].reshape(32, LANES).astype(BF16)

    loads[3].wait()
    lay_v(0, core)
    give_v.wait()
    lay_v(1, other)

    lane = lax.broadcasted_iota(jnp.int32, (256, LANES), 1)
    low = (lane < 64) == (core == 0)
    me = (row * NX + x) * 2 + core

    def s1_copy(q, tx, c):
        return pltpu.make_async_remote_copy(
            src_ref=sbuf.at[q, tx * 2 + c],
            dst_ref=s1.at[me],
            send_sem=ssend.at[q, tx * 2 + c],
            recv_sem=srecv.at[me],
            device_id=at(z, tx, c, q),
            device_id_type=MESH,
        )

    def quarter(step, carry):
        high = lax.rem(lax.div(z, 4) + 1 - lax.div(step, 2), 2)
        below = lax.rem(lax.div(z, 2) + step + lax.div(step, 2), 2)
        q = 2 * high + below

        def arrived(i, inner):
            source = q * 8 + i
            pltpu.make_async_copy(recv.at[source], recv.at[source], trecv.at[source]).wait()
            return inner

        lax.fori_loop(0, 8, arrived, 0)
        tf[...] = recv[pl.ds(q * 8, 8)].reshape(1024, LANES).astype(F32)
        for d in range(16):
            value = tf[pl.ds(d, 64, stride=16), :].astype(BF16)
            tmat[0:64, d * LANES : (d + 1) * LANES] = value
            tmat[64:128, d * LANES : (d + 1) * LANES] = value
        product = lax.dot_general(
            vmat[...], tmat[...], (((1,), (1,)), ((), ())), preferred_element_type=F32
        )
        sbuf[q] = jnp.where(low, product[:256], product[256:]).reshape(8, 32, LANES)
        for dx in X_ORDER:
            for dc in range(2):
                tx = around(dx)
                c = lax.rem(core + dc, 2)
                if (dx, dc) == (0, 0):

                    @pl.when(q == row)
                    def _():
                        s1[me] = sbuf[q, tx * 2 + c]

                    @pl.when(q != row)
                    def _():
                        s1_copy(q, tx, c).start()

                else:
                    s1_copy(q, tx, c).start()
        return carry

    lax.fori_loop(0, NY, quarter, 0)

    def s1_wait(i, carry):
        slot = lax.rem(me + i, 32)
        pltpu.make_async_copy(s1.at[slot], s1.at[slot], srecv.at[slot]).wait()
        return carry

    lax.fori_loop(1, 32, s1_wait, 0)
    from0, from1 = s1[0], s1[1]
    for i in range(2, 32, 2):
        from0 = from0 + s1[i]
        from1 = from1 + s1[i + 1]
    first = lax.broadcasted_iota(jnp.int32, (32, LANES), 1) < 64
    msg[0:4] = jnp.where(first, from0, from1).reshape(4, 8, LANES)
    msg[4:8] = jnp.where(first, from1, from0).reshape(4, 8, LANES)

    def block(tz):
        return pltpu.make_async_remote_copy(
            src_ref=msg.at[tz], dst_ref=fin.at[z], send_sem=msend.at[tz], recv_sem=mrecv.at[z],
            device_id=at(tz, x, core, row), device_id_type=MESH,
        )

    blocks = [block(lax.rem(z + dz, NZ)) for dz in (4, 3, 5, 2, 6, 1, 7)]
    for copy in blocks:
        copy.start()
    fin[z] = msg[z]
    for dz in (1, 7, 2, 6, 3, 5, 4):
        source = lax.rem(z + dz, NZ)
        pltpu.make_async_copy(fin.at[source], fin.at[source], mrecv.at[source]).wait()
    total = fin[0]
    for i in range(1, NZ):
        total = total + fin[i]

    source = lax.broadcasted_iota(jnp.int32, (LANES, LANES), 0)
    target_lane = lax.broadcasted_iota(jnp.int32, (LANES, LANES), 1)
    half = jnp.where(source < 64, 0, 1)
    source_core = jnp.where(z < 4, half, 1 - half)
    inside = source - 64 * half
    target = 16 * lax.div(inside, 8) + 8 * source_core + lax.rem(inside, 8)
    move = jnp.where(target == target_lane, 1.0, 0.0).astype(F32)
    result = lax.dot_general(
        total, move, (((1,), (0,)), ((), ())), preferred_element_type=F32, precision=lax.Precision.HIGHEST
    )
    irrep_b8 = label_of(col * 8 + lax.broadcasted_iota(jnp.int32, (8, LANES), 0))
    live = jnp.bitwise_xor(irrep_b8, irrep_a) == pair_ref[pl.ds(row, 1), :]
    out_ref[...] = jnp.where(live, result, 0.0)

    for copy in chunks + blocks:
        copy.wait_send()

    def s_left(i, carry):
        slot = lax.rem(me + i, 32)
        s1_copy(lax.div(slot, 8), lax.div(lax.rem(slot, 8), 2), lax.rem(slot, 2)).wait_send()
        return carry

    lax.fori_loop(1, 32, s_left, 0)


def on_device(amplitudes, integrals, virtual_irrep, pair_irrep):
    v = integrals.reshape(512 * 8, LANES)
    hbm = pl.BlockSpec(memory_space=pltpu.HBM)
    out = pl.pallas_call(
        kernel,
        out_shape=jax.ShapeDtypeStruct((8, LANES), F32),
        in_specs=[hbm, hbm, hbm, hbm],
        out_specs=pl.BlockSpec(memory_space=pltpu.VMEM),
        scratch_shapes=[
            pltpu.VMEM((8, 512, LANES), BF16),
            pltpu.VMEM((4, LANES), jnp.int32),
            pltpu.VMEM((4, LANES), jnp.int32),
            pltpu.VMEM((CHIPS, 8, 16, LANES), BF16),
            pltpu.VMEM((2, 4096, LANES), BF16),
            pltpu.VMEM((4096, LANES), F32),
            pltpu.VMEM((512, 2048), BF16),
            pltpu.VMEM((1024, LANES), F32),
            pltpu.VMEM((128, 2048), BF16),
            pltpu.VMEM((4, 8, 32, LANES), F32),
            pltpu.VMEM((32, 32, LANES), F32),
            pltpu.VMEM((8, 8, LANES), F32),
            pltpu.VMEM((8, 8, LANES), F32),
            pltpu.SemaphoreType.DMA((3,)),
            pltpu.SemaphoreType.DMA((CHIPS,)),
            pltpu.SemaphoreType.DMA((CHIPS,)),
            pltpu.SemaphoreType.DMA((3,)),
            pltpu.SemaphoreType.DMA((4, 8)),
            pltpu.SemaphoreType.DMA((32,)),
            pltpu.SemaphoreType.DMA((NZ,)),
            pltpu.SemaphoreType.DMA((NZ,)),
        ],
        compiler_params=pltpu.CompilerParams(
            collective_id=0, has_side_effects=True, vmem_limit_bytes=63 * 1024 * 1024
        ),
        name="ladder",
    )(amplitudes, v, virtual_irrep.reshape(4, LANES), pair_irrep.reshape(4, LANES))
    return out.reshape(8, 1, LANES)


def solution(mesh):
    in_specs = (P("col", None, "row"), P(None, None, "col", "row"), P(), P())
    out_specs = P("col", None, "row")
    return jax.shard_map(on_device, mesh=mesh, in_specs=in_specs, out_specs=out_specs, check_vma=False)
```

```python
import jax
import jax.numpy as jnp
from jax import lax
from jax.experimental import pallas as pl
from jax.experimental.pallas import tpu as pltpu
from jax.sharding import PartitionSpec as P

MESH = pl.DeviceIdType.MESH
F32 = jnp.float32
BF16 = jnp.bfloat16
NZ, NX, NY = 8, 4, 4
CHIPS = NZ * NX
LANES = 128
IRREPS = 4
WINDOW = 2
FAR = (2, 1, 3, 0)


def kernel(
    t_hbm, v_hbm, virt_hbm, pair_hbm, out_ref,
    tsrc, virt_ref, pair_ref, recv, vbuf, vf, vmat, tf, tmat, sbuf, s1, msg, fin, move,
    lsem, tsend, trecv, vsem, ssend, srecv, msend, mrecv,
):
    row = lax.axis_index("row")
    col = lax.axis_index("col")
    core = lax.rem(col, 2)
    chip = lax.div(col, 2)
    z = lax.div(chip, NX)
    x = lax.rem(chip, NX)
    other = 1 - core

    for i in range(8):
        pltpu.make_async_copy(t_hbm.at[i], tsrc.at[:, i], lsem.at[0]).start()
    loads = [
        pltpu.make_async_copy(virt_hbm, virt_ref, lsem.at[1]),
        pltpu.make_async_copy(pair_hbm, pair_ref, lsem.at[2]),
        pltpu.make_async_copy(v_hbm, vbuf.at[0], vsem.at[0]),
    ]
    for load in loads:
        load.start()

    def around(dx):
        return lax.rem(x + dx, NX)

    def at(z_index, x_index, core_index, row_index):
        return {"row": row_index, "col": (z_index * NX + x_index) * 2 + core_index}

    def up(dz):
        return lax.rem(z + dz, NZ)

    mates = set()
    for d1 in range(NZ):
        mates |= {(d1, d2, 0, 0) for d2 in range(NX)}
    mates |= {(0, d1, d2, d3) for d1 in range(NX) for d2 in range(2) for d3 in range(NY)}
    mates.remove((0, 0, 0, 0))

    def far(mate):
        dz, dx, dc, dy = mate
        return (-min(dz, NZ - dz) - min(dx, NX - dx) - min(dy, NY - dy), mate)

    mates = sorted(mates, key=far)
    barrier = pltpu.get_barrier_semaphore()
    for dz, dx, dc, dy in mates:
        mate = at(up(dz), around(dx), lax.rem(core + dc, 2), lax.rem(row + dy, NY))
        pl.semaphore_signal(barrier, inc=1, device_id=mate, device_id_type=MESH)
    met = len(mates)
    pltpu.make_async_copy(tsrc, tsrc, lsem.at[0]).wait()
    pl.semaphore_wait(barrier, met)

    def distances(p):
        return 4 - p, p + 4 * lax.div(p + 3, 4)

    def chunk(p, side, dx):
        tz = lax.rem(z + NZ - distances(p)[side], NZ)
        tx = around(dx)
        return pltpu.make_async_remote_copy(
            src_ref=tsrc.at[tz * NX + tx],
            dst_ref=recv.at[p, side * NX + x],
            send_sem=tsend.at[p],
            recv_sem=trecv.at[p],
            device_id=at(tz, tx, core, row),
            device_id_type=MESH,
        )

    def send_phase(p):
        for dx in FAR:
            for side in range(2):
                if (side, dx) == (1, 0):

                    @pl.when(p != 0)
                    def _():
                        chunk(p, side, dx).start()

                else:
                    chunk(p, side, dx).start()

    own_t = pltpu.make_async_copy(tsrc.at[chip], recv.at[0, NX + x], trecv.at[0])
    for p in range(WINDOW):
        send_phase(p)
    own_t.start()
    give_v = pltpu.make_async_remote_copy(
        src_ref=v_hbm, dst_ref=vbuf.at[1], send_sem=vsem.at[1], recv_sem=vsem.at[2],
        device_id=at(z, x, other, row), device_id_type=MESH,
    )
    give_v.start()

    loads[0].wait()
    loads[1].wait()
    labels = virt_ref[...]
    starts = []
    for n in range(1, IRREPS):
        below = jnp.where(labels < n, 1.0, 0.0).astype(F32)
        starts.append(jnp.sum(jnp.sum(below, axis=1, keepdims=True), axis=0, keepdims=True))

    def label_of(place):
        place = place.astype(F32)
        total = jnp.zeros(place.shape, jnp.int32)
        for start in starts:
            total = total + jnp.where(place >= start, 1, 0)
        return total

    irrep_a = label_of(jnp.zeros((1, LANES), jnp.int32))
    irrep_c = virt_ref[pl.ds(row, 1), :]
    irrep_b = label_of(lax.broadcasted_iota(jnp.int32, (512, LANES), 0))

    def lay_v(half, from_core):
        def widen(i, carry):
            rows = pl.ds(pl.multiple_of(i * 512, 512), 512)
            vf[rows, :] = vbuf[half, rows, :].astype(F32)
            return carry

        lax.fori_loop(0, 8, widen, 0)

        for d in range(8):
            place = chip * 16 + from_core * 8 + d
            irrep_d = label_of(jnp.full((1, LANES), 1, jnp.int32) * place)
            want = jnp.bitwise_xor(jnp.bitwise_xor(irrep_d, irrep_c), irrep_a)
            value = vf[pl.ds(d, 512, stride=8), :]
            value = jnp.where(irrep_b == want, value, 0.0)
            value = value.reshape(4, 2, NX, 2, 8, LANES)
            lanes = pl.ds(pl.multiple_of((from_core * 8 + d) * LANES, LANES), LANES)
            for h in range(4):
                for tx in range(NX):
                    for c in range(2):
                        at_row = h * 128 + (tx * 2 + c) * 16
                        vmat[at_row : at_row + 16, lanes] = value[h, :, tx, c].reshape(16, LANES).astype(BF16)

    source = lax.broadcasted_iota(jnp.int32, (LANES, LANES), 0)
    target_lane = lax.broadcasted_iota(jnp.int32, (LANES, LANES), 1)
    origin = lax.rem(lax.div(source, 32) + 4 - lax.div(z, 2), 4)
    target = 64 * lax.div(origin, 2) + 16 * lax.div(lax.rem(source, 32), 8) + 8 * lax.rem(origin, 2) + lax.rem(source, 8)
    move[...] = jnp.where(target == target_lane, 1.0, 0.0).astype(F32)

    loads[2].wait()
    lay_v(0, core)
    give_v.wait()
    lay_v(1, other)

    lane_group = lax.div(lax.broadcasted_iota(jnp.int32, (LANES, LANES), 1), 32)
    me = (row * NX + x) * 2 + core

    def s1_copy(p, side, tx, c):
        plane = up(distances(p)[side])
        return pltpu.make_async_remote_copy(
            src_ref=sbuf.at[p, side, tx * 2 + c],
            dst_ref=s1.at[lax.rem(plane, 2), me],
            send_sem=ssend.at[0],
            recv_sem=srecv.at[0],
            device_id=at(z, tx, c, lax.div(plane, 2)),
            device_id_type=MESH,
        )

    def phase(p, carry):
        @pl.when(p == 0)
        def _():
            pltpu.make_async_copy(recv.at[0, 0:7], recv.at[0, 0:7], tsend.at[0]).wait()

        @pl.when(p != 0)
        def _():
            pltpu.make_async_copy(recv.at[p], recv.at[p], tsend.at[p]).wait()

        @pl.when(p + WINDOW < NY)
        def _():
            send_phase(p + WINDOW)

        pltpu.make_async_copy(recv.at[p], recv.at[p], trecv.at[p]).wait()
        tf[...] = recv[p].reshape(1024, LANES).astype(F32)
        for d in range(16):
            value = tf[pl.ds(d, 64, stride=16), :].astype(BF16)
            for side in range(2):
                for copies in range(4):
                    at_row = side * 128 + copies * 32
                    tmat[at_row : at_row + 32, d * LANES : (d + 1) * LANES] = value[side * 32 : side * 32 + 32]
        product = lax.dot_general(
            vmat[...], tmat[...], (((1,), (1,)), ((), ())), preferred_element_type=F32
        )
        for side in range(2):
            plane = up(distances(p)[side])
            turn = 2 * lax.rem(plane, 2) + core
            packed = product[0:128, side * LANES : (side + 1) * LANES]
            for h in range(1, 4):
                mine = lane_group == lax.rem(h + turn, 4)
                packed = jnp.where(mine, product[h * 128 : h * 128 + 128, side * LANES : (side + 1) * LANES], packed)
            sbuf[p, side] = packed.reshape(8, 16, LANES)
            q = lax.div(plane, 2)
            for dx in FAR:
                for dc in (1, 0):
                    tx = around(dx)
                    c = lax.rem(core + dc, 2)
                    if (dx, dc) == (0, 0):

                        @pl.when(q == row)
                        def _():
                            pltpu.make_async_copy(
                                sbuf.at[p, side, tx * 2 + c], s1.at[lax.rem(plane, 2), me], srecv.at[0]
                            ).start()

                        @pl.when(q != row)
                        def _():
                            s1_copy(p, side, tx, c).start()

                    else:
                        s1_copy(p, side, tx, c).start()
        return carry

    lax.fori_loop(0, NY, phase, 0)

    pltpu.make_async_copy(s1, s1, srecv.at[0]).wait()
    sums = []
    for parity in range(2):
        for c in range(2):
            total = s1[parity, c]
            for i in range(c + 2, 32, 2):
                total = total + s1[parity, i]
            sums.append(total)
    group = lax.div(lax.broadcasted_iota(jnp.int32, (16, LANES), 1), 32)
    for h in range(4):
        merged = sums[0]
        for k in range(1, 4):
            merged = jnp.where(group == (h + k) % 4, sums[k], merged)
        msg[2 * h : 2 * h + 2] = merged.reshape(2, 8, LANES)

    def block(dz):
        return pltpu.make_async_remote_copy(
            src_ref=msg.at[up(dz)], dst_ref=fin.at[z], send_sem=msend.at[0], recv_sem=mrecv.at[0],
            device_id=at(up(dz), x, core, row), device_id_type=MESH,
        )

    for dz in (4, 3, 5, 2, 6, 1, 7):
        block(dz).start()
    pltpu.make_async_copy(msg.at[z], fin.at[z], mrecv.at[0]).start()
    pltpu.make_async_copy(fin, fin, mrecv.at[0]).wait()
    total = fin[0]
    for i in range(1, NZ):
        total = total + fin[i]
    result = lax.dot_general(
        total, move[...], (((1,), (0,)), ((), ())), preferred_element_type=F32, precision=lax.Precision.HIGHEST
    )
    irrep_b8 = label_of(col * 8 + lax.broadcasted_iota(jnp.int32, (8, LANES), 0))
    live = jnp.bitwise_xor(irrep_b8, irrep_a) == pair_ref[pl.ds(row, 1), :]
    out_ref[...] = jnp.where(live, result, 0.0)

    pltpu.make_async_copy(fin.at[0:7], fin.at[0:7], msend.at[0]).wait()
    pltpu.make_async_copy(s1.at[0], s1.at[0], ssend.at[0]).wait()
    pltpu.make_async_copy(s1.at[0, 0:30], s1.at[0, 0:30], ssend.at[0]).wait()


def on_device(amplitudes, integrals, virtual_irrep, pair_irrep):
    v = integrals.reshape(512 * 8, LANES)
    hbm = pl.BlockSpec(memory_space=pltpu.HBM)
    out = pl.pallas_call(
        kernel,
        out_shape=jax.ShapeDtypeStruct((8, LANES), F32),
        in_specs=[hbm, hbm, hbm, hbm],
        out_specs=pl.BlockSpec(memory_space=pltpu.VMEM),
        scratch_shapes=[
            pltpu.VMEM((CHIPS, 8, 16, LANES), BF16),
            pltpu.VMEM((4, LANES), jnp.int32),
            pltpu.VMEM((4, LANES), jnp.int32),
            pltpu.VMEM((4, 8, 8, 16, LANES), BF16),
            pltpu.VMEM((2, 4096, LANES), BF16),
            pltpu.VMEM((4096, LANES), F32),
            pltpu.VMEM((512, 2048), BF16),
            pltpu.VMEM((1024, LANES), F32),
            pltpu.VMEM((256, 2048), BF16),
            pltpu.VMEM((4, 2, 8, 16, LANES), F32),
            pltpu.VMEM((2, 32, 16, LANES), F32),
            pltpu.VMEM((8, 8, LANES), F32),
            pltpu.VMEM((8, 8, LANES), F32),
            pltpu.VMEM((LANES, LANES), F32),
            pltpu.SemaphoreType.DMA((3,)),
            pltpu.SemaphoreType.DMA((4,)),
            pltpu.SemaphoreType.DMA((4,)),
            pltpu.SemaphoreType.DMA((3,)),
            pltpu.SemaphoreType.DMA((1,)),
            pltpu.SemaphoreType.DMA((1,)),
            pltpu.SemaphoreType.DMA((1,)),
            pltpu.SemaphoreType.DMA((1,)),
        ],
        compiler_params=pltpu.CompilerParams(
            collective_id=0, has_side_effects=True, vmem_limit_bytes=63 * 1024 * 1024
        ),
        name="ladder",
    )(amplitudes.reshape(8, CHIPS, 16, LANES), v, virtual_irrep.reshape(4, LANES), pair_irrep.reshape(4, LANES))
    return out.reshape(8, 1, LANES)


def solution(mesh):
    in_specs = (P("col", None, "row"), P(None, None, "col", "row"), P(), P())
    out_specs = P("col", None, "row")
    return jax.shard_map(on_device, mesh=mesh, in_specs=in_specs, out_specs=out_specs, check_vma=False)
```

```python
import jax
import jax.numpy as jnp
from jax import lax
from jax.experimental import pallas as pl
from jax.experimental.pallas import tpu as pltpu
from jax.sharding import PartitionSpec as P

MESH = pl.DeviceIdType.MESH
F32 = jnp.float32
BF16 = jnp.bfloat16
NZ, NX, NY = 8, 4, 4
CHIPS = NZ * NX
LANES = 128
IRREPS = 4
WINDOW = 2
OWN = 2
FAR = (2, 1, 3, 0)


def kernel(
    t_hbm, v_hbm, virt_hbm, pair_hbm, out_ref,
    tsrc, virt_ref, pair_ref, recv, vbuf, vf, vmat, tf, tmat, sbuf, s1, msg, fin, move,
    lsem, tsend, trecv, vsem, ssend, srecv, msend, mrecv, pass_z, pass_y,
):
    row = lax.axis_index("row")
    col = lax.axis_index("col")
    core = lax.rem(col, 2)
    chip = lax.div(col, 2)
    z = lax.div(chip, NX)
    x = lax.rem(chip, NX)
    other = 1 - core

    def around(dx):
        return lax.rem(x + dx, NX)

    def at(z_index, x_index, core_index, row_index):
        return {"row": row_index, "col": (z_index * NX + x_index) * 2 + core_index}

    def up(dz):
        return lax.rem(z + dz, NZ)

    mates = [(dz, dx, 0, 0) for dx in FAR for dz in (1, NZ - 1, 0) if (dz, dx) != (0, 0)]
    mates += [(0, 0, 0, dy) for dy in (2, 1, 3)] + [(0, 0, 1, 0)]
    barrier = pltpu.get_barrier_semaphore()

    def mate_at(dz, dx, dc, dy):
        return at(up(dz), around(dx), lax.rem(core + dc, 2), lax.rem(row + dy, NY))

    for mate in mates:
        pl.semaphore_signal(barrier, inc=1, device_id=mate_at(*mate), device_id_type=MESH)
    met = len(mates)
    for i in range(8):
        pltpu.make_async_copy(t_hbm.at[i], tsrc.at[:, i], lsem.at[0]).start()
    loads = [
        pltpu.make_async_copy(virt_hbm, virt_ref, lsem.at[1]),
        pltpu.make_async_copy(pair_hbm, pair_ref, lsem.at[2]),
        pltpu.make_async_copy(v_hbm, vbuf.at[0], vsem.at[0]),
    ]
    for load in loads:
        load.start()
    pltpu.make_async_copy(tsrc, tsrc, lsem.at[0]).wait()
    pl.semaphore_wait(barrier, met)

    def distances(p):
        is1 = lax.div(p + 3, 4) - lax.div(p + 2, 4)
        is2 = lax.div(p + 2, 4) - lax.div(p + 1, 4)
        is3 = lax.div(p + 1, 4)
        side_a = 1 + 2 * is1 + 3 * is2 + is3
        return side_a, (NZ - side_a) * (1 - is2)

    def chunk(p, side, dx):
        tz = lax.rem(z + NZ - distances(p)[side], NZ)
        tx = around(dx)
        return pltpu.make_async_remote_copy(
            src_ref=tsrc.at[tz * NX + tx],
            dst_ref=recv.at[p, side * NX + x],
            send_sem=tsend.at[p],
            recv_sem=trecv.at[p],
            device_id=at(tz, tx, core, row),
            device_id_type=MESH,
        )

    def send_phase(p):
        for dx in FAR:
            for side in range(2):
                if (side, dx) == (1, 0):

                    @pl.when(p != OWN)
                    def _():
                        chunk(p, side, dx).start()

                else:
                    chunk(p, side, dx).start()

    own_t = pltpu.make_async_copy(tsrc.at[chip], recv.at[OWN, NX + x], trecv.at[OWN])
    send_phase(0)

    around_z = [(1, 0, 0, 0), (NZ - 1, 0, 0, 0)]
    in_chip_column = [(0, 0, 0, 2), (0, 0, 0, 1), (0, 0, 0, 3), (0, 0, 1, 0)]

    def pass_on(turn):
        told = [(pass_z, mate) for mate in around_z]
        if turn < 2:
            told += [(pass_y, mate) for mate in in_chip_column]
        for semaphore, mate in told:
            pl.semaphore_signal(semaphore.at[turn], inc=1, device_id=mate_at(*mate), device_id_type=MESH)
        pl.semaphore_wait(pass_z.at[turn], 2)
        if turn < 2:
            pl.semaphore_wait(pass_y.at[turn], 4)

    pass_on(0)
    pass_on(1)
    send_phase(1)
    pass_on(2)
    own_t.start()
    give_v = pltpu.make_async_remote_copy(
        src_ref=v_hbm, dst_ref=vbuf.at[1], send_sem=vsem.at[1], recv_sem=vsem.at[2],
        device_id=at(z, x, other, row), device_id_type=MESH,
    )
    give_v.start()

    loads[0].wait()
    loads[1].wait()
    labels = virt_ref[...]
    starts = []
    for n in range(1, IRREPS):
        below = jnp.where(labels < n, 1.0, 0.0).astype(F32)
        starts.append(jnp.sum(jnp.sum(below, axis=1, keepdims=True), axis=0, keepdims=True))

    def label_of(place):
        place = place.astype(F32)
        total = jnp.zeros(place.shape, jnp.int32)
        for start in starts:
            total = total + jnp.where(place >= start, 1, 0)
        return total

    irrep_a = label_of(jnp.zeros((1, LANES), jnp.int32))
    irrep_c = virt_ref[pl.ds(row, 1), :]
    irrep_b = label_of(lax.broadcasted_iota(jnp.int32, (512, LANES), 0))

    def lay_v(half, from_core):
        def widen(i, carry):
            rows = pl.ds(pl.multiple_of(i * 512, 512), 512)
            vf[rows, :] = vbuf[half, rows, :].astype(F32)
            return carry

        lax.fori_loop(0, 8, widen, 0)

        for d in range(8):
            place = chip * 16 + from_core * 8 + d
            irrep_d = label_of(jnp.full((1, LANES), 1, jnp.int32) * place)
            want = jnp.bitwise_xor(jnp.bitwise_xor(irrep_d, irrep_c), irrep_a)
            value = vf[pl.ds(d, 512, stride=8), :]
            value = jnp.where(irrep_b == want, value, 0.0)
            value = value.reshape(4, 2, NX, 2, 8, LANES)
            lanes = pl.ds(pl.multiple_of((from_core * 8 + d) * LANES, LANES), LANES)
            for h in range(4):
                for tx in range(NX):
                    for c in range(2):
                        at_row = h * 128 + (tx * 2 + c) * 16
                        vmat[at_row : at_row + 16, lanes] = value[h, :, tx, c].reshape(16, LANES).astype(BF16)

    to = lax.broadcasted_iota(jnp.int32, (8, LANES), 1)
    group_of = lax.rem(2 * lax.div(to, 64) + lax.rem(lax.div(to, 8), 2) + lax.div(z, 2), 4)
    move[0] = 32 * group_of + 8 * lax.rem(lax.div(to, 16), 4) + lax.rem(to, 8)
    irrep_b8 = label_of(col * 8 + lax.broadcasted_iota(jnp.int32, (8, LANES), 0))
    live = jnp.bitwise_xor(irrep_b8, irrep_a) == pair_ref[pl.ds(row, 1), :]
    move[1] = jnp.where(live, 1, 0)

    loads[2].wait()
    lay_v(0, core)
    give_v.wait()
    lay_v(1, other)

    lane_group = lax.div(lax.broadcasted_iota(jnp.int32, (LANES, LANES), 1), 32)
    me = (row * NX + x) * 2 + core

    def s1_copy(p, side, tx, c):
        plane = up(distances(p)[side])
        return pltpu.make_async_remote_copy(
            src_ref=sbuf.at[p, side, tx * 2 + c],
            dst_ref=s1.at[lax.rem(plane, 2), me],
            send_sem=ssend.at[0],
            recv_sem=srecv.at[0],
            device_id=at(z, tx, c, lax.div(plane, 2)),
            device_id_type=MESH,
        )

    def phase(p, carry):
        @pl.when(p == OWN)
        def _():
            pltpu.make_async_copy(recv.at[p, 0:7], recv.at[p, 0:7], tsend.at[p]).wait()

        @pl.when(p != OWN)
        def _():
            pltpu.make_async_copy(recv.at[p], recv.at[p], tsend.at[p]).wait()

        @pl.when(p + WINDOW < NY)
        def _():
            send_phase(p + WINDOW)

        pltpu.make_async_copy(recv.at[p], recv.at[p], trecv.at[p]).wait()
        tf[...] = recv[p].reshape(1024, LANES).astype(F32)
        for d in range(16):
            value = tf[pl.ds(d, 64, stride=16), :].astype(BF16)
            for side in range(2):
                for copies in range(4):
                    at_row = side * 128 + copies * 32
                    tmat[at_row : at_row + 32, d * LANES : (d + 1) * LANES] = value[side * 32 : side * 32 + 32]
        product = lax.dot_general(
            vmat[...], tmat[...], (((1,), (1,)), ((), ())), preferred_element_type=F32
        )
        for side in range(2):
            plane = up(distances(p)[side])
            turn = 2 * lax.rem(plane, 2) + core
            packed = product[0:128, side * LANES : (side + 1) * LANES]
            for h in range(1, 4):
                mine = lane_group == lax.rem(h + turn, 4)
                packed = jnp.where(mine, product[h * 128 : h * 128 + 128, side * LANES : (side + 1) * LANES], packed)
            sbuf[p, side] = packed.reshape(8, 16, LANES)
            q = lax.div(plane, 2)
            for dx in FAR:
                for dc in (1, 0):
                    tx = around(dx)
                    c = lax.rem(core + dc, 2)
                    if (dx, dc) == (0, 0):

                        @pl.when(q == row)
                        def _():
                            pltpu.make_async_copy(
                                sbuf.at[p, side, tx * 2 + c], s1.at[lax.rem(plane, 2), me], srecv.at[0]
                            ).start()

                        @pl.when(q != row)
                        def _():
                            s1_copy(p, side, tx, c).start()

                    else:
                        s1_copy(p, side, tx, c).start()
        return carry

    lax.fori_loop(0, NY, phase, 0)

    pltpu.make_async_copy(s1, s1, srecv.at[0]).wait()
    sums = []
    for parity in range(2):
        for c in range(2):
            total = s1[parity, c]
            for i in range(c + 2, 32, 2):
                total = total + s1[parity, i]
            sums.append(total)
    group = lax.div(lax.broadcasted_iota(jnp.int32, (16, LANES), 1), 32)
    for h in range(4):
        merged = sums[0]
        for k in range(1, 4):
            merged = jnp.where(group == (h + k) % 4, sums[k], merged)
        msg[2 * h : 2 * h + 2] = merged.reshape(2, 8, LANES)

    def block(dz):
        return pltpu.make_async_remote_copy(
            src_ref=msg.at[up(dz)], dst_ref=fin.at[z], send_sem=msend.at[0], recv_sem=mrecv.at[0],
            device_id=at(up(dz), x, core, row), device_id_type=MESH,
        )

    for dz in (4, 3, 5, 2, 6, 1, 7):
        block(dz).start()
    pltpu.make_async_copy(msg.at[z], fin.at[z], mrecv.at[0]).start()
    pltpu.make_async_copy(fin, fin, mrecv.at[0]).wait()
    total = fin[0]
    for i in range(1, NZ):
        total = total + fin[i]
    result = jnp.take_along_axis(total, move[0], axis=1)
    out_ref[...] = jnp.where(move[1] == 1, result, 0.0)

    pltpu.make_async_copy(fin.at[0:7], fin.at[0:7], msend.at[0]).wait()
    pltpu.make_async_copy(s1.at[0], s1.at[0], ssend.at[0]).wait()
    pltpu.make_async_copy(s1.at[0, 0:30], s1.at[0, 0:30], ssend.at[0]).wait()


def on_device(amplitudes, integrals, virtual_irrep, pair_irrep):
    v = integrals.reshape(512 * 8, LANES)
    hbm = pl.BlockSpec(memory_space=pltpu.HBM)
    out = pl.pallas_call(
        kernel,
        out_shape=jax.ShapeDtypeStruct((8, LANES), F32),
        in_specs=[hbm, hbm, hbm, hbm],
        out_specs=pl.BlockSpec(memory_space=pltpu.VMEM),
        scratch_shapes=[
            pltpu.VMEM((CHIPS, 8, 16, LANES), BF16),
            pltpu.VMEM((4, LANES), jnp.int32),
            pltpu.VMEM((4, LANES), jnp.int32),
            pltpu.VMEM((4, 8, 8, 16, LANES), BF16),
            pltpu.VMEM((2, 4096, LANES), BF16),
            pltpu.VMEM((4096, LANES), F32),
            pltpu.VMEM((512, 2048), BF16),
            pltpu.VMEM((1024, LANES), F32),
            pltpu.VMEM((256, 2048), BF16),
            pltpu.VMEM((4, 2, 8, 16, LANES), F32),
            pltpu.VMEM((2, 32, 16, LANES), F32),
            pltpu.VMEM((8, 8, LANES), F32),
            pltpu.VMEM((8, 8, LANES), F32),
            pltpu.VMEM((2, 8, LANES), jnp.int32),
            pltpu.SemaphoreType.DMA((3,)),
            pltpu.SemaphoreType.DMA((4,)),
            pltpu.SemaphoreType.DMA((4,)),
            pltpu.SemaphoreType.DMA((3,)),
            pltpu.SemaphoreType.DMA((1,)),
            pltpu.SemaphoreType.DMA((1,)),
            pltpu.SemaphoreType.DMA((1,)),
            pltpu.SemaphoreType.DMA((1,)),
            pltpu.SemaphoreType.REGULAR((3,)),
            pltpu.SemaphoreType.REGULAR((2,)),
        ],
        compiler_params=pltpu.CompilerParams(
            collective_id=0, has_side_effects=True, vmem_limit_bytes=63 * 1024 * 1024
        ),
        name="ladder",
    )(amplitudes.reshape(8, CHIPS, 16, LANES), v, virtual_irrep.reshape(4, LANES), pair_irrep.reshape(4, LANES))
    return out.reshape(8, 1, LANES)


def solution(mesh):
    in_specs = (P("col", None, "row"), P(None, None, "col", "row"), P(), P())
    out_specs = P("col", None, "row")
    return jax.shard_map(on_device, mesh=mesh, in_specs=in_specs, out_specs=out_specs, check_vma=False)
```

```python
import jax
import jax.numpy as jnp
from jax import lax
from jax.experimental import pallas as pl
from jax.experimental.pallas import tpu as pltpu
from jax.sharding import PartitionSpec as P

MESH = pl.DeviceIdType.MESH
F32 = jnp.float32
BF16 = jnp.bfloat16
NZ, NX, NY = 8, 4, 4
CHIPS = NZ * NX
LANES = 128
IRREPS = 4
WINDOW = 2
OWN = 2
FAR = (2, 1, 3, 0)


def kernel(
    t_hbm, v_hbm, virt_hbm, pair_hbm, out_ref,
    tsrc, virt_ref, pair_ref, recv, vbuf, vf, vmat, tf, tmat, sbuf, s1, msg, fin, move,
    lsem, tsend, trecv, vsem, ssend, srecv, msend, mrecv, pass_z, pass_y,
):
    row = lax.axis_index("row")
    col = lax.axis_index("col")
    core = lax.rem(col, 2)
    chip = lax.div(col, 2)
    z = lax.div(chip, NX)
    x = lax.rem(chip, NX)
    other = 1 - core

    def around(dx):
        return lax.rem(x + dx, NX)

    def at(z_index, x_index, core_index, row_index):
        return {"row": row_index, "col": (z_index * NX + x_index) * 2 + core_index}

    def up(dz):
        return lax.rem(z + dz, NZ)

    mates = [(dz, dx, 0, 0) for dx in FAR for dz in (1, NZ - 1, 0) if (dz, dx) != (0, 0)]
    mates += [(0, 0, 0, dy) for dy in (2, 1, 3)] + [(0, 0, 1, 0)]
    barrier = pltpu.get_barrier_semaphore()

    def mate_at(dz, dx, dc, dy):
        return at(up(dz), around(dx), lax.rem(core + dc, 2), lax.rem(row + dy, NY))

    for mate in mates:
        pl.semaphore_signal(barrier, inc=1, device_id=mate_at(*mate), device_id_type=MESH)
    met = len(mates)
    for i in range(8):
        pltpu.make_async_copy(t_hbm.at[i], tsrc.at[:, i], lsem.at[0]).start()
    loads = [
        pltpu.make_async_copy(virt_hbm, virt_ref, lsem.at[1]),
        pltpu.make_async_copy(pair_hbm, pair_ref, lsem.at[2]),
        pltpu.make_async_copy(v_hbm, vbuf.at[0], vsem.at[0]),
    ]
    for load in loads:
        load.start()
    pltpu.make_async_copy(tsrc, tsrc, lsem.at[0]).wait()
    pl.semaphore_wait(barrier, met)

    def distances(p):
        is1 = lax.div(p + 3, 4) - lax.div(p + 2, 4)
        is2 = lax.div(p + 2, 4) - lax.div(p + 1, 4)
        is3 = lax.div(p + 1, 4)
        side_a = 1 + 2 * is1 + 3 * is2 + is3
        return side_a, (NZ - side_a) * (1 - is2)

    def chunk(p, side, dx):
        tz = lax.rem(z + NZ - distances(p)[side], NZ)
        tx = around(dx)
        return pltpu.make_async_remote_copy(
            src_ref=tsrc.at[tz * NX + tx],
            dst_ref=recv.at[p, side * NX + x],
            send_sem=tsend.at[p],
            recv_sem=trecv.at[p],
            device_id=at(tz, tx, core, row),
            device_id_type=MESH,
        )

    def send_phase(p):
        for dx in FAR:
            for side in range(2):
                if (side, dx) == (1, 0):

                    @pl.when(p != OWN)
                    def _():
                        chunk(p, side, dx).start()

                else:
                    chunk(p, side, dx).start()

    own_t = pltpu.make_async_copy(tsrc.at[chip], recv.at[OWN, NX + x], trecv.at[OWN])
    send_phase(0)

    around_z = [(1, 0, 0, 0), (NZ - 1, 0, 0, 0)]
    in_chip_column = [(0, 0, 0, 2), (0, 0, 0, 1), (0, 0, 0, 3), (0, 0, 1, 0)]

    def pass_on(turn):
        told = [(pass_z, mate) for mate in around_z]
        if turn < 2:
            told += [(pass_y, mate) for mate in in_chip_column]
        for semaphore, mate in told:
            pl.semaphore_signal(semaphore.at[turn], inc=1, device_id=mate_at(*mate), device_id_type=MESH)
        pl.semaphore_wait(pass_z.at[turn], 2)
        if turn < 2:
            pl.semaphore_wait(pass_y.at[turn], 4)

    pass_on(0)
    pass_on(1)
    send_phase(1)
    pass_on(2)
    own_t.start()
    give_v = pltpu.make_async_remote_copy(
        src_ref=v_hbm, dst_ref=vbuf.at[1], send_sem=vsem.at[1], recv_sem=vsem.at[2],
        device_id=at(z, x, other, row), device_id_type=MESH,
    )
    give_v.start()

    loads[0].wait()
    loads[1].wait()
    labels = virt_ref[...]
    starts = []
    for n in range(1, IRREPS):
        below = jnp.where(labels < n, 1.0, 0.0).astype(F32)
        starts.append(jnp.sum(jnp.sum(below, axis=1, keepdims=True), axis=0, keepdims=True))

    def label_of(place):
        place = place.astype(F32)
        total = jnp.zeros(place.shape, jnp.int32)
        for start in starts:
            total = total + jnp.where(place >= start, 1, 0)
        return total

    irrep_a = label_of(jnp.zeros((1, LANES), jnp.int32))
    irrep_c = virt_ref[pl.ds(row, 1), :]
    irrep_b = label_of(lax.broadcasted_iota(jnp.int32, (512, LANES), 0))

    def lay_v(half, from_core):
        def widen(i, carry):
            rows = pl.ds(pl.multiple_of(i * 512, 512), 512)
            vf[rows, :] = vbuf[half, rows, :].astype(F32)
            return carry

        lax.fori_loop(0, 8, widen, 0)

        for d in range(8):
            place = chip * 16 + from_core * 8 + d
            irrep_d = label_of(jnp.full((1, LANES), 1, jnp.int32) * place)
            want = jnp.bitwise_xor(jnp.bitwise_xor(irrep_d, irrep_c), irrep_a)
            value = vf[pl.ds(d, 512, stride=8), :]
            value = jnp.where(irrep_b == want, value, 0.0)
            value = value.reshape(4, 2, NX, 2, 8, LANES)
            lanes = pl.ds(pl.multiple_of((from_core * 8 + d) * LANES, LANES), LANES)
            for h in range(4):
                for tx in range(NX):
                    for c in range(2):
                        at_row = h * 128 + (tx * 2 + c) * 16
                        vmat[at_row : at_row + 16, lanes] = value[h, :, tx, c].reshape(16, LANES).astype(BF16)

    to = lax.broadcasted_iota(jnp.int32, (8, LANES), 1)
    group_of = lax.rem(2 * lax.div(to, 64) + lax.rem(lax.div(to, 8), 2) + lax.div(z, 2), 4)
    move[0] = 32 * group_of + 8 * lax.rem(lax.div(to, 16), 4) + lax.rem(to, 8)
    irrep_b8 = label_of(col * 8 + lax.broadcasted_iota(jnp.int32, (8, LANES), 0))
    live = jnp.bitwise_xor(irrep_b8, irrep_a) == pair_ref[pl.ds(row, 1), :]
    move[1] = jnp.where(live, 1, 0)

    loads[2].wait()
    lay_v(0, core)
    give_v.wait()
    lay_v(1, other)

    lane_group = lax.div(lax.broadcasted_iota(jnp.int32, (LANES, LANES), 1), 32)
    me = (row * NX + x) * 2 + core

    def s1_copy(p, side, tx, c):
        plane = up(distances(p)[side])
        return pltpu.make_async_remote_copy(
            src_ref=sbuf.at[p, side, tx * 2 + c],
            dst_ref=s1.at[lax.rem(plane, 2), me],
            send_sem=ssend.at[0],
            recv_sem=srecv.at[0],
            device_id=at(z, tx, c, lax.div(plane, 2)),
            device_id_type=MESH,
        )

    def phase(p, carry):
        @pl.when(p == OWN)
        def _():
            pltpu.make_async_copy(recv.at[p, 0:7], recv.at[p, 0:7], tsend.at[p]).wait()

        @pl.when(p != OWN)
        def _():
            pltpu.make_async_copy(recv.at[p], recv.at[p], tsend.at[p]).wait()

        @pl.when(p + WINDOW < NY)
        def _():
            send_phase(p + WINDOW)

        pltpu.make_async_copy(recv.at[p], recv.at[p], trecv.at[p]).wait()
        tf[...] = recv[p].reshape(1024, LANES).astype(F32)
        for d in range(16):
            value = tf[pl.ds(d, 64, stride=16), :].astype(BF16)
            for side in range(2):
                for copies in range(4):
                    at_row = side * 128 + copies * 32
                    tmat[at_row : at_row + 32, d * LANES : (d + 1) * LANES] = value[side * 32 : side * 32 + 32]
        product = lax.dot_general(
            vmat[...], tmat[...], (((1,), (1,)), ((), ())), preferred_element_type=F32
        )
        for side in range(2):
            plane = up(distances(p)[side])
            turn = 2 * lax.rem(plane, 2) + core
            packed = product[0:128, side * LANES : (side + 1) * LANES]
            for h in range(1, 4):
                mine = lane_group == lax.rem(h + turn, 4)
                packed = jnp.where(mine, product[h * 128 : h * 128 + 128, side * LANES : (side + 1) * LANES], packed)
            sbuf[p, side] = packed.reshape(8, 16, LANES)
            q = lax.div(plane, 2)
            for dx in FAR:
                for dc in (1, 0):
                    tx = around(dx)
                    c = lax.rem(core + dc, 2)
                    if (dx, dc) == (0, 0):

                        @pl.when(q == row)
                        def _():
                            pltpu.make_async_copy(
                                sbuf.at[p, side, tx * 2 + c], s1.at[lax.rem(plane, 2), me], srecv.at[0]
                            ).start()

                        @pl.when(q != row)
                        def _():
                            s1_copy(p, side, tx, c).start()

                    else:
                        s1_copy(p, side, tx, c).start()
        return carry

    lax.fori_loop(0, NY, phase, 0)

    pltpu.make_async_copy(s1, s1, srecv.at[0]).wait()
    sums = []
    for parity in range(2):
        for c in range(2):
            total = s1[parity, c]
            for i in range(c + 2, 32, 2):
                total = total + s1[parity, i]
            sums.append(total)
    group = lax.div(lax.broadcasted_iota(jnp.int32, (16, LANES), 1), 32)
    for h in range(4):
        merged = sums[0]
        for k in range(1, 4):
            merged = jnp.where(group == (h + k) % 4, sums[k], merged)
        msg[2 * h : 2 * h + 2] = merged.reshape(2, 8, LANES)

    def block(dz):
        return pltpu.make_async_remote_copy(
            src_ref=msg.at[up(dz)], dst_ref=fin.at[z], send_sem=msend.at[0], recv_sem=mrecv.at[0],
            device_id=at(up(dz), x, core, row), device_id_type=MESH,
        )

    for dz in (4, 3, 5, 2, 6, 1, 7):
        block(dz).start()
    pltpu.make_async_copy(msg.at[z], fin.at[z], mrecv.at[0]).start()
    pltpu.make_async_copy(fin, fin, mrecv.at[0]).wait()
    total = fin[0]
    for i in range(1, NZ):
        total = total + fin[i]
    result = jnp.take_along_axis(total, move[0], axis=1)
    out_ref[...] = jnp.where(move[1] == 1, result, 0.0)

    pltpu.make_async_copy(fin.at[0:7], fin.at[0:7], msend.at[0]).wait()
    pltpu.make_async_copy(s1.at[0], s1.at[0], ssend.at[0]).wait()
    pltpu.make_async_copy(s1.at[0, 0:30], s1.at[0, 0:30], ssend.at[0]).wait()


def on_device(amplitudes, integrals, virtual_irrep, pair_irrep):
    v = integrals.reshape(512 * 8, LANES)
    hbm = pl.BlockSpec(memory_space=pltpu.HBM)
    out = pl.pallas_call(
        kernel,
        out_shape=jax.ShapeDtypeStruct((8, LANES), F32),
        in_specs=[hbm, hbm, hbm, hbm],
        out_specs=pl.BlockSpec(memory_space=pltpu.VMEM),
        scratch_shapes=[
            pltpu.VMEM((CHIPS, 8, 16, LANES), BF16),
            pltpu.VMEM((4, LANES), jnp.int32),
            pltpu.VMEM((4, LANES), jnp.int32),
            pltpu.VMEM((4, 8, 8, 16, LANES), BF16),
            pltpu.VMEM((2, 4096, LANES), BF16),
            pltpu.VMEM((4096, LANES), F32),
            pltpu.VMEM((512, 2048), BF16),
            pltpu.VMEM((1024, LANES), F32),
            pltpu.VMEM((256, 2048), BF16),
            pltpu.VMEM((4, 2, 8, 16, LANES), F32),
            pltpu.VMEM((2, 32, 16, LANES), F32),
            pltpu.VMEM((8, 8, LANES), F32),
            pltpu.VMEM((8, 8, LANES), F32),
            pltpu.VMEM((2, 8, LANES), jnp.int32),
            pltpu.SemaphoreType.DMA((3,)),
            pltpu.SemaphoreType.DMA((4,)),
            pltpu.SemaphoreType.DMA((4,)),
            pltpu.SemaphoreType.DMA((3,)),
            pltpu.SemaphoreType.DMA((1,)),
            pltpu.SemaphoreType.DMA((1,)),
            pltpu.SemaphoreType.DMA((1,)),
            pltpu.SemaphoreType.DMA((1,)),
            pltpu.SemaphoreType.REGULAR((3,)),
            pltpu.SemaphoreType.REGULAR((2,)),
        ],
        compiler_params=pltpu.CompilerParams(
            collective_id=0, has_side_effects=True, vmem_limit_bytes=53 * 1024 * 1024
        ),
        name="ladder",
    )(amplitudes.reshape(8, CHIPS, 16, LANES), v, virtual_irrep.reshape(4, LANES), pair_irrep.reshape(4, LANES))
    return out.reshape(8, 1, LANES)


def solution(mesh):
    in_specs = (P("col", None, "row"), P(None, None, "col", "row"), P(), P())
    out_specs = P("col", None, "row")
    return jax.shard_map(on_device, mesh=mesh, in_specs=in_specs, out_specs=out_specs, check_vma=False)
```

```python
import jax
import jax.numpy as jnp
from jax import lax
from jax.experimental import pallas as pl
from jax.experimental.pallas import tpu as pltpu
from jax.sharding import PartitionSpec as P

MESH = pl.DeviceIdType.MESH
F32 = jnp.float32
BF16 = jnp.bfloat16
NZ, NX, NY = 8, 4, 4
CHIPS = NZ * NX
LANES = 128
IRREPS = 4
WINDOW = 3
OWN = 2
FAR = (2, 1, 3, 0)


def kernel(
    t_hbm, v_hbm, virt_hbm, pair_hbm, out_ref,
    tsrc, virt_ref, pair_ref, recv, vbuf, vf, vmat, tf, tmat, sbuf, s1, msg, fin, move,
    lsem, tsend, trecv, vsem, ssend, srecv, msend, mrecv, pass_z, pass_y,
):
    row = lax.axis_index("row")
    col = lax.axis_index("col")
    core = lax.rem(col, 2)
    chip = lax.div(col, 2)
    z = lax.div(chip, NX)
    x = lax.rem(chip, NX)
    other = 1 - core

    def around(dx):
        return lax.rem(x + dx, NX)

    def at(z_index, x_index, core_index, row_index):
        return {"row": row_index, "col": (z_index * NX + x_index) * 2 + core_index}

    def up(dz):
        return lax.rem(z + dz, NZ)

    mates = [(dz, dx, 0, 0) for dx in FAR for dz in (1, NZ - 1, 0) if (dz, dx) != (0, 0)]
    mates += [(0, 0, 0, dy) for dy in (2, 1, 3)] + [(0, 0, 1, 0)]
    barrier = pltpu.get_barrier_semaphore()

    def mate_at(dz, dx, dc, dy):
        return at(up(dz), around(dx), lax.rem(core + dc, 2), lax.rem(row + dy, NY))

    for mate in mates:
        pl.semaphore_signal(barrier, inc=1, device_id=mate_at(*mate), device_id_type=MESH)
    met = len(mates)
    for i in range(8):
        pltpu.make_async_copy(t_hbm.at[i], tsrc.at[:, i], lsem.at[0]).start()
    loads = [
        pltpu.make_async_copy(virt_hbm, virt_ref, lsem.at[1]),
        pltpu.make_async_copy(pair_hbm, pair_ref, lsem.at[2]),
        pltpu.make_async_copy(v_hbm, vbuf.at[0], vsem.at[0]),
    ]
    for load in loads:
        load.start()
    pltpu.make_async_copy(tsrc, tsrc, lsem.at[0]).wait()
    pl.semaphore_wait(barrier, met)

    def distances(p):
        is1 = lax.div(p + 3, 4) - lax.div(p + 2, 4)
        is2 = lax.div(p + 2, 4) - lax.div(p + 1, 4)
        is3 = lax.div(p + 1, 4)
        side_a = 1 + 2 * is1 + 3 * is2 + is3
        return side_a, (NZ - side_a) * (1 - is2)

    def chunk(p, side, dx):
        tz = lax.rem(z + NZ - distances(p)[side], NZ)
        tx = around(dx)
        return pltpu.make_async_remote_copy(
            src_ref=tsrc.at[tz * NX + tx],
            dst_ref=recv.at[p, side * NX + x],
            send_sem=tsend.at[p],
            recv_sem=trecv.at[p],
            device_id=at(tz, tx, core, row),
            device_id_type=MESH,
        )

    def send_phase(p):
        for dx in FAR:
            for side in range(2):
                if (side, dx) == (1, 0):

                    @pl.when(p != OWN)
                    def _():
                        chunk(p, side, dx).start()

                else:
                    chunk(p, side, dx).start()

    own_t = pltpu.make_async_copy(tsrc.at[chip], recv.at[OWN, NX + x], trecv.at[OWN])
    send_phase(0)

    around_z = [(1, 0, 0, 0), (NZ - 1, 0, 0, 0)]
    in_chip_column = [(0, 0, 0, 2), (0, 0, 0, 1), (0, 0, 0, 3), (0, 0, 1, 0)]

    def pass_on(turn):
        told = [(pass_z, mate) for mate in around_z]
        if turn < 2:
            told += [(pass_y, mate) for mate in in_chip_column]
        for semaphore, mate in told:
            pl.semaphore_signal(semaphore.at[turn], inc=1, device_id=mate_at(*mate), device_id_type=MESH)
        pl.semaphore_wait(pass_z.at[turn], 2)
        if turn < 2:
            pl.semaphore_wait(pass_y.at[turn], 4)

    pass_on(0)
    pass_on(1)
    send_phase(1)
    pass_on(2)
    for p in range(2, WINDOW):
        send_phase(p)
    own_t.start()
    give_v = pltpu.make_async_remote_copy(
        src_ref=v_hbm, dst_ref=vbuf.at[1], send_sem=vsem.at[1], recv_sem=vsem.at[2],
        device_id=at(z, x, other, row), device_id_type=MESH,
    )
    give_v.start()

    loads[0].wait()
    loads[1].wait()
    labels = virt_ref[...]
    starts = []
    for n in range(1, IRREPS):
        below = jnp.where(labels < n, 1.0, 0.0).astype(F32)
        starts.append(jnp.sum(jnp.sum(below, axis=1, keepdims=True), axis=0, keepdims=True))

    def label_of(place):
        place = place.astype(F32)
        total = jnp.zeros(place.shape, jnp.int32)
        for start in starts:
            total = total + jnp.where(place >= start, 1, 0)
        return total

    irrep_a = label_of(jnp.zeros((1, LANES), jnp.int32))
    irrep_c = virt_ref[pl.ds(row, 1), :]
    irrep_b = label_of(lax.broadcasted_iota(jnp.int32, (512, LANES), 0))

    def lay_v(half, from_core):
        def widen(i, carry):
            rows = pl.ds(pl.multiple_of(i * 512, 512), 512)
            vf[rows, :] = vbuf[half, rows, :].astype(F32)
            return carry

        lax.fori_loop(0, 8, widen, 0)

        for d in range(8):
            place = chip * 16 + from_core * 8 + d
            irrep_d = label_of(jnp.full((1, LANES), 1, jnp.int32) * place)
            want = jnp.bitwise_xor(jnp.bitwise_xor(irrep_d, irrep_c), irrep_a)
            value = vf[pl.ds(d, 512, stride=8), :]
            value = jnp.where(irrep_b == want, value, 0.0)
            value = value.reshape(4, 2, NX, 2, 8, LANES)
            lanes = pl.ds(pl.multiple_of((from_core * 8 + d) * LANES, LANES), LANES)
            for h in range(4):
                for tx in range(NX):
                    for c in range(2):
                        at_row = h * 128 + (tx * 2 + c) * 16
                        vmat[at_row : at_row + 16, lanes] = value[h, :, tx, c].reshape(16, LANES).astype(BF16)

    to = lax.broadcasted_iota(jnp.int32, (8, LANES), 1)
    group_of = lax.rem(2 * lax.div(to, 64) + lax.rem(lax.div(to, 8), 2) + lax.div(z, 2), 4)
    move[0] = 32 * group_of + 8 * lax.rem(lax.div(to, 16), 4) + lax.rem(to, 8)
    irrep_b8 = label_of(col * 8 + lax.broadcasted_iota(jnp.int32, (8, LANES), 0))
    live = jnp.bitwise_xor(irrep_b8, irrep_a) == pair_ref[pl.ds(row, 1), :]
    move[1] = jnp.where(live, 1, 0)

    loads[2].wait()
    lay_v(0, core)
    give_v.wait()
    lay_v(1, other)

    lane_group = lax.div(lax.broadcasted_iota(jnp.int32, (LANES, LANES), 1), 32)
    me = (row * NX + x) * 2 + core

    def s1_copy(p, side, tx, c):
        plane = up(distances(p)[side])
        return pltpu.make_async_remote_copy(
            src_ref=sbuf.at[p, side, tx * 2 + c],
            dst_ref=s1.at[lax.rem(plane, 2), me],
            send_sem=ssend.at[0],
            recv_sem=srecv.at[0],
            device_id=at(z, tx, c, lax.div(plane, 2)),
            device_id_type=MESH,
        )

    def phase(p, carry):
        @pl.when(p == OWN)
        def _():
            pltpu.make_async_copy(recv.at[p, 0:7], recv.at[p, 0:7], tsend.at[p]).wait()

        @pl.when(p != OWN)
        def _():
            pltpu.make_async_copy(recv.at[p], recv.at[p], tsend.at[p]).wait()

        @pl.when(p + WINDOW < NY)
        def _():
            send_phase(p + WINDOW)

        pltpu.make_async_copy(recv.at[p], recv.at[p], trecv.at[p]).wait()
        tf[...] = recv[p].reshape(1024, LANES).astype(F32)
        for d in range(16):
            value = tf[pl.ds(d, 64, stride=16), :].astype(BF16)
            for side in range(2):
                for copies in range(4):
                    at_row = side * 128 + copies * 32
                    tmat[at_row : at_row + 32, d * LANES : (d + 1) * LANES] = value[side * 32 : side * 32 + 32]
        product = lax.dot_general(
            vmat[...], tmat[...], (((1,), (1,)), ((), ())), preferred_element_type=F32
        )
        for side in range(2):
            plane = up(distances(p)[side])
            turn = 2 * lax.rem(plane, 2) + core
            packed = product[0:128, side * LANES : (side + 1) * LANES]
            for h in range(1, 4):
                mine = lane_group == lax.rem(h + turn, 4)
                packed = jnp.where(mine, product[h * 128 : h * 128 + 128, side * LANES : (side + 1) * LANES], packed)
            sbuf[p, side] = packed.reshape(8, 16, LANES)
            q = lax.div(plane, 2)
            for dx in FAR:
                for dc in (1, 0):
                    tx = around(dx)
                    c = lax.rem(core + dc, 2)
                    if (dx, dc) == (0, 0):

                        @pl.when(q == row)
                        def _():
                            pltpu.make_async_copy(
                                sbuf.at[p, side, tx * 2 + c], s1.at[lax.rem(plane, 2), me], srecv.at[0]
                            ).start()

                        @pl.when(q != row)
                        def _():
                            s1_copy(p, side, tx, c).start()

                    else:
                        s1_copy(p, side, tx, c).start()
        return carry

    lax.fori_loop(0, NY, phase, 0)

    pltpu.make_async_copy(s1, s1, srecv.at[0]).wait()
    sums = []
    for parity in range(2):
        for c in range(2):
            total = s1[parity, c]
            for i in range(c + 2, 32, 2):
                total = total + s1[parity, i]
            sums.append(total)
    group = lax.div(lax.broadcasted_iota(jnp.int32, (16, LANES), 1), 32)
    for h in range(4):
        merged = sums[0]
        for k in range(1, 4):
            merged = jnp.where(group == (h + k) % 4, sums[k], merged)
        msg[2 * h : 2 * h + 2] = merged.reshape(2, 8, LANES)

    def block(dz):
        return pltpu.make_async_remote_copy(
            src_ref=msg.at[up(dz)], dst_ref=fin.at[z], send_sem=msend.at[0], recv_sem=mrecv.at[0],
            device_id=at(up(dz), x, core, row), device_id_type=MESH,
        )

    for dz in (4, 3, 5, 2, 6, 1, 7):
        block(dz).start()
    pltpu.make_async_copy(msg.at[z], fin.at[z], mrecv.at[0]).start()
    pltpu.make_async_copy(fin, fin, mrecv.at[0]).wait()
    total = fin[0]
    for i in range(1, NZ):
        total = total + fin[i]
    result = jnp.take_along_axis(total, move[0], axis=1)
    out_ref[...] = jnp.where(move[1] == 1, result, 0.0)

    pltpu.make_async_copy(fin.at[0:7], fin.at[0:7], msend.at[0]).wait()
    pltpu.make_async_copy(s1.at[0], s1.at[0], ssend.at[0]).wait()
    pltpu.make_async_copy(s1.at[0, 0:30], s1.at[0, 0:30], ssend.at[0]).wait()


def on_device(amplitudes, integrals, virtual_irrep, pair_irrep):
    v = integrals.reshape(512 * 8, LANES)
    hbm = pl.BlockSpec(memory_space=pltpu.HBM)
    out = pl.pallas_call(
        kernel,
        out_shape=jax.ShapeDtypeStruct((8, LANES), F32),
        in_specs=[hbm, hbm, hbm, hbm],
        out_specs=pl.BlockSpec(memory_space=pltpu.VMEM),
        scratch_shapes=[
            pltpu.VMEM((CHIPS, 8, 16, LANES), BF16),
            pltpu.VMEM((4, LANES), jnp.int32),
            pltpu.VMEM((4, LANES), jnp.int32),
            pltpu.VMEM((4, 8, 8, 16, LANES), BF16),
            pltpu.VMEM((2, 4096, LANES), BF16),
            pltpu.VMEM((4096, LANES), F32),
            pltpu.VMEM((512, 2048), BF16),
            pltpu.VMEM((1024, LANES), F32),
            pltpu.VMEM((256, 2048), BF16),
            pltpu.VMEM((4, 2, 8, 16, LANES), F32),
            pltpu.VMEM((2, 32, 16, LANES), F32),
            pltpu.VMEM((8, 8, LANES), F32),
            pltpu.VMEM((8, 8, LANES), F32),
            pltpu.VMEM((2, 8, LANES), jnp.int32),
            pltpu.SemaphoreType.DMA((3,)),
            pltpu.SemaphoreType.DMA((4,)),
            pltpu.SemaphoreType.DMA((4,)),
            pltpu.SemaphoreType.DMA((3,)),
            pltpu.SemaphoreType.DMA((1,)),
            pltpu.SemaphoreType.DMA((1,)),
            pltpu.SemaphoreType.DMA((1,)),
            pltpu.SemaphoreType.DMA((1,)),
            pltpu.SemaphoreType.REGULAR((3,)),
            pltpu.SemaphoreType.REGULAR((2,)),
        ],
        compiler_params=pltpu.CompilerParams(
            collective_id=0, has_side_effects=True, vmem_limit_bytes=53 * 1024 * 1024
        ),
        name="ladder",
    )(amplitudes.reshape(8, CHIPS, 16, LANES), v, virtual_irrep.reshape(4, LANES), pair_irrep.reshape(4, LANES))
    return out.reshape(8, 1, LANES)


def solution(mesh):
    in_specs = (P("col", None, "row"), P(None, None, "col", "row"), P(), P())
    out_specs = P("col", None, "row")
    return jax.shard_map(on_device, mesh=mesh, in_specs=in_specs, out_specs=out_specs, check_vma=False)
```
